32 devices in a mesh: dp: 8 (over z, x), chan: 4 (over y, core).
Axes of the slice: x: 2, y: 2, z: 4, core: 2. Of those that a mesh axis runs over, the one named last changes fastest.
Arguments:
- pixels: bfloat16 [13888, 2016], P('dp', 'chan'), may hold values from -6 to 6
- wa1: bfloat16 [2016, 2016], P(None, 'chan'), may hold values from -0.125 to 0.125
- wb1: bfloat16 [9, 56, 2016], P(None, None, 'chan'), may hold values from -0.25 to 0.25
- se_down1: bfloat16 [2016, 504], P('chan'), may hold values from -0.125 to 0.125
- se_bias1: float32 [504], replicated, may hold values from -4 to 4
- se_up1: bfloat16 [504, 2016], P(None, 'chan'), may hold values from -0.25 to 0.25
- se_gate_bias1: float32 [2016], P('chan'), may hold values from -6 to 6
- wc1: bfloat16 [2016, 2016], P('chan'), may hold values from -0.375 to 0.375
- wp1: bfloat16 [2016, 2016], P(None, 'chan'), may hold values from -0.125 to 0.125
- scales1: float32 [4, 2016], P(None, 'chan'), may hold values from 0.5 to 1.5
- shifts1: float32 [4, 2016], P(None, 'chan'), may hold values from -3 to 3
- wa2: bfloat16 [2016, 2016], P(None, 'chan'), may hold values from -0.125 to 0.125
- wb2: bfloat16 [9, 56, 2016], P(None, None, 'chan'), may hold values from -0.25 to 0.25
- se_down2: bfloat16 [2016, 504], P('chan'), may hold values from -0.125 to 0.125
- se_bias2: float32 [504], replicated, may hold values from -4 to 4
- se_up2: bfloat16 [504, 2016], P(None, 'chan'), may hold values from -0.25 to 0.25
- se_gate_bias2: float32 [2016], P('chan'), may hold values from -6 to 6
- wc2: bfloat16 [2016, 2016], P('chan'), may hold values from -0.375 to 0.375
- scales2: float32 [3, 2016], P(None, 'chan'), may hold values from 0.5 to 1.5
- shifts2: float32 [3, 2016], P(None, 'chan'), may hold values from -3 to 3
- prototypes: bfloat16 [2016, 3000], P('chan'), may hold values from -0.8984375 to 0.8984375
- live_counts: int32 [24], P('dp'), may hold values from 1 to 5, as said below
- crop_image: int32 [80], P('dp'), may hold values from 0 to 3
- codes: int32 [32], P('dp'), may hold values from 0 to 2999
Outputs:
- block_out: bfloat16 [3472, 2016], P('dp', 'chan')
- crop_loss: float32 [80], P('dp')
- pixels_grad: bfloat16 [13888, 2016], P('dp', 'chan')
- grad_wa1: float32 [2016, 2016], P(None, 'chan')
- grad_wb1: float32 [9, 56, 2016], P(None, None, 'chan')
- grad_se_down1: float32 [2016, 504], P('chan')
- grad_se_bias1: float32 [504], replicated
- grad_se_up1: float32 [504, 2016], P(None, 'chan')
- grad_se_gate_bias1: float32 [2016], P('chan')
- grad_wc1: float32 [2016, 2016], P('chan')
- grad_wp1: float32 [2016, 2016], P(None, 'chan')
- grad_scales1: float32 [4, 2016], P(None, 'chan')
- grad_shifts1: float32 [4, 2016], P(None, 'chan')
- grad_wa2: float32 [2016, 2016], P(None, 'chan')
- grad_wb2: float32 [9, 56, 2016], P(None, None, 'chan')
- grad_se_down2: float32 [2016, 504], P('chan')
- grad_se_bias2: float32 [504], replicated
- grad_se_up2: float32 [504, 2016], P(None, 'chan')
- grad_se_gate_bias2: float32 [2016], P('chan')
- grad_wc2: float32 [2016, 2016], P('chan')
- grad_scales2: float32 [3, 2016], P(None, 'chan')
- grad_shifts2: float32 [3, 2016], P(None, 'chan')
The draws below stay inside these ranges and needn't reach their ends.
Inputs may be any that keep to these rules, and one draw needn't show every extreme that they name: `live_counts`: entry 3 d + k is how many of index d's slots of bucket k (k = 0, 1, 2 for sides 10, 14, 18) are live, the first ones; it never passes that bucket's slots (5, 3, 2), and in every draw each bucket is full on some index of dp.
All inputs are finite; a program needn't handle non-finite values.
Results may differ from the reference program's by a relative error of at most 0.017.
Values may be sent and summed in bfloat16 or wider, within the bound.
A program may use at most 320 MiB of HBM per device.

```python
import jax
import jax.numpy as jnp
from jax import lax

D = 2016
GW = 56
HID = 504
PROTOS = 3000
C10 = 5
C14 = 3
C18 = 2
IMG_DEV = 4
PIX = 13888
CROPS = 80
IMAGES = 32
N_DP = 8


def draw_live_counts(key, part):
    first_key, second_key = jax.random.split(jax.random.fold_in(key, 17))
    limits = jnp.array([C10, C14, C18], jnp.int32)
    raw = jax.random.randint(first_key, (N_DP, 3), 0, 1 << 20) % limits[None, :] + 1
    full_rank = jax.random.randint(second_key, (3,), 0, N_DP)
    chosen = jnp.arange(N_DP, dtype=jnp.int32)[:, None] == full_rank[None, :]
    return jnp.where(chosen, limits[None, :], raw).reshape(-1).astype(jnp.int32)


def set_ends(entries, own_key, smallest, largest):
    spot = [jax.random.randint(jax.random.fold_in(own_key, axis), (), 0, length) for axis, length in enumerate(entries.shape)]
    longest = entries.shape.index(max(entries.shape))
    beside = spot[:longest] + [(spot[longest] + 1) % entries.shape[longest]] + spot[longest + 1:]
    return entries.at[tuple(spot)].set(smallest).at[tuple(beside)].set(largest)


def steps_of(stream_key, shape, cuts, low, largest):
    def one(axis_at, blocks):
        steps = jax.random.uniform(jax.random.fold_in(jax.random.fold_in(stream_key, 6), axis_at), (blocks,), jnp.float32, low / len(cuts), largest / len(cuts))
        return jnp.repeat(jnp.exp(steps), shape[axis_at] // blocks).reshape((-1,) + (1,) * (len(shape) - axis_at - 1))

    gain = one(*cuts[0])
    for cut in cuts[1:]:
        gain = gain * one(*cut)
    return gain


def centred(own_key, dims, scale, limit, cuts=(), kind=jnp.bfloat16):
    result = scale * jax.random.normal(own_key, dims, jnp.float32)
    if cuts:
        result = result * steps_of(own_key, dims, cuts, -0.22, 0.18)
    return jnp.clip(result, -limit, limit).astype(kind)


def setup_inputs(seed: int = 0) -> dict:
    key_list = jax.random.split(jax.random.key(seed), 25)
    pixels = centred(key_list[0], (PIX, D), 1.0, 6.0, ((0, 8), (1, 4)))
    wa1 = centred(key_list[1], (D, D), D ** -0.5, 0.125, ((1, 4),))
    wb1 = centred(key_list[2], (9, GW, D), (9 * GW) ** -0.5, 0.25, ((2, 4),))
    se_down1 = centred(key_list[3], (D, HID), D ** -0.5, 0.125, ((0, 4),))
    se_bias1 = centred(key_list[4], (HID,), 0.3, 4.0, (), jnp.float32)
    se_up1 = centred(key_list[5], (HID, D), HID ** -0.5, 0.25, ((1, 4),))
    se_gate_bias1 = centred(key_list[6], (D,), 0.5, 6.0, ((0, 4),), jnp.float32)
    wc1 = centred(key_list[7], (D, D), (D // 8) ** -0.5, 0.375, ((0, 4),))
    wp1 = centred(key_list[8], (D, D), D ** -0.5, 0.125, ((1, 4),))
    scales1 = jnp.clip(1.0 + 0.1 * jax.random.normal(key_list[9], (4, D), jnp.float32), 0.5, 1.5)
    shifts1 = centred(key_list[10], (4, D), 0.2, 3.0, ((1, 4),), jnp.float32)
    wa2 = centred(key_list[11], (D, D), D ** -0.5, 0.125, ((1, 4),))
    wb2 = centred(key_list[12], (9, GW, D), (9 * GW) ** -0.5, 0.25, ((2, 4),))
    se_down2 = centred(key_list[13], (D, HID), D ** -0.5, 0.125, ((0, 4),))
    se_bias2 = centred(key_list[14], (HID,), 0.3, 4.0, (), jnp.float32)
    se_up2 = centred(key_list[15], (HID, D), HID ** -0.5, 0.25, ((1, 4),))
    se_gate_bias2 = centred(key_list[16], (D,), 0.5, 6.0, ((0, 4),), jnp.float32)
    wc2 = centred(key_list[17], (D, D), (D // 8) ** -0.5, 0.375, ((0, 4),))
    scales2 = jnp.clip(1.0 + 0.1 * jax.random.normal(key_list[18], (3, D), jnp.float32), 0.5, 1.5)
    shifts2 = centred(key_list[19], (3, D), 0.2, 3.0, ((1, 4),), jnp.float32)
    prototypes = centred(key_list[20], (D, PROTOS), 0.15, 0.8984375, ((0, 4),))
    live_counts = draw_live_counts(jax.random.fold_in(key_list[24], 71), 0)
    crop_image = set_ends(jax.random.randint(key_list[22], (CROPS,), 0, IMG_DEV), jax.random.fold_in(key_list[22], 1), 0, IMG_DEV - 1).astype(jnp.int32)
    codes = set_ends(jax.random.randint(key_list[23], (IMAGES,), 0, PROTOS), jax.random.fold_in(key_list[23], 1), 0, PROTOS - 1).astype(jnp.int32)
    return {"pixels": pixels, "wa1": wa1, "wb1": wb1, "se_down1": se_down1, "se_bias1": se_bias1, "se_up1": se_up1, "se_gate_bias1": se_gate_bias1, "wc1": wc1, "wp1": wp1, "scales1": scales1, "shifts1": shifts1, "wa2": wa2, "wb2": wb2, "se_down2": se_down2, "se_bias2": se_bias2, "se_up2": se_up2, "se_gate_bias2": se_gate_bias2, "wc2": wc2, "scales2": scales2, "shifts2": shifts2, "prototypes": prototypes, "live_counts": live_counts, "crop_image": crop_image, "codes": codes}


@jax.custom_vjp
def low(v):
    return lax.optimization_barrier(v.astype(jnp.bfloat16)).astype(jnp.float32)

@jax.custom_vjp
def low_back(v):
    return v

def low_keep(v):
    return (low(v), None)

def low_pass(kept, grad):
    return (grad,)

def back_keep(v):
    return (v, None)

def back_low(kept, grad):
    return (low(grad),)
low.defvjp(low_keep, low_pass)
low_back.defvjp(back_keep, back_low)
exact_arithmetic_mode = lax.Precision.HIGHEST
crop_sides = (10, 14, 18)
loss_scale = 256.0
logit_sharpness_divisor = 0.1

def split_crops(flat, sides):
    width = flat.shape[-1]
    per_device = flat.reshape(N_DP, -1, width)
    pieces = []
    offset = 0
    for count, side in zip((C10, C14, C18), sides):
        length = count * side * side
        pieces.append(per_device[:, offset:offset + length].reshape(N_DP * count, side, side, width))
        offset += length
    return pieces

def join_crops(pieces):
    width = pieces[0].shape[-1]
    rows = [piece.reshape(N_DP, -1, width) for piece in pieces]
    return jnp.concatenate(rows, axis=1).reshape(-1, width)

def project(field, weight):
    return jnp.einsum('nhwc,cd->nhwd', field, weight, precision=exact_arithmetic_mode)

def grouped_conv(field, weight, stride):
    kernel = weight.reshape(3, 3, GW, D)
    return lax.conv_general_dilated(field, kernel, (stride, stride), ((1, 1), (1, 1)), dimension_numbers=('NHWC', 'HWIO', 'NHWC'), feature_group_count=D // GW, precision=exact_arithmetic_mode)

def block(pieces, weights, stride):
    w_first, w_grouped, w_down, b_down, w_up, b_up, w_last, w_short, gains, shifts = weights
    results = []
    for field in pieces:
        first = low_back(project(field, w_first))
        first_act = low(jax.nn.silu(gains[0] * first + shifts[0]))
        grouped = low_back(grouped_conv(first_act, w_grouped, stride))
        grouped_act = jax.nn.silu(gains[1] * grouped + shifts[1])
        pooled = lax.optimization_barrier(jnp.mean(grouped_act, axis=(1, 2)))
        hidden = jax.nn.silu(jnp.dot(pooled, w_down, precision=exact_arithmetic_mode) + b_down)
        gating = jax.nn.sigmoid(jnp.dot(hidden, w_up, precision=exact_arithmetic_mode) + b_up)
        excited = low(grouped_act * gating[:, None, None, :])
        branch = low_back(project(excited, w_last))
        if stride == 2:
            short = low_back(project(field[:, ::2, ::2], w_short))
            residual = gains[3] * short + shifts[3]
        else:
            residual = field
        results.append(jax.nn.silu(gains[2] * branch + shifts[2] + residual))
    return results

def reference(pixels, wa1, wb1, se_down1, se_bias1, se_up1, se_gate_bias1, wc1, wp1, scales1, shifts1, wa2, wb2, se_down2, se_bias2, se_up2, se_gate_bias2, wc2, scales2, shifts2, prototypes, live_counts, crop_image, codes):
    counts = live_counts.reshape(N_DP, 3)
    lives = []
    for bucket, count in enumerate((C10, C14, C18)):
        lives.append((jnp.arange(count, dtype=jnp.int32)[None, :] < counts[:, bucket:bucket + 1]).astype(jnp.float32))
    live = jnp.concatenate(lives, axis=1).reshape(-1)
    target = jnp.take_along_axis(codes.reshape(N_DP, IMG_DEV), crop_image.reshape(N_DP, C10 + C14 + C18), axis=1).reshape(-1)
    cluster_center_codes = prototypes.astype(jnp.float32)

    def objective(pixel_values, *weight_values):
        first_weights = weight_values[:10]
        second_weights = (weight_values[10], weight_values[11], weight_values[12], weight_values[13], weight_values[14], weight_values[15], weight_values[16], None, weight_values[17], weight_values[18])
        pieces = split_crops(pixel_values, crop_sides)
        after_one = [low(piece) for piece in block(pieces, first_weights, 2)]
        after_two = block(after_one, second_weights, 1)
        embeds = [lax.optimization_barrier(jnp.mean(piece, axis=(1, 2))).reshape(N_DP, -1, D) for piece in after_two]
        feature_code_lines = jnp.concatenate(embeds, axis=1).reshape(-1, D)
        euclidean_length = jnp.sqrt(lax.optimization_barrier(jnp.sum(feature_code_lines * feature_code_lines, axis=1)) + 1e-06)
        similarity_table = jnp.dot(feature_code_lines, cluster_center_codes, precision=exact_arithmetic_mode) / (logit_sharpness_divisor * euclidean_length[:, None])
        picked = jnp.take_along_axis(similarity_table, target[:, None], axis=1)[:, 0]
        ce = jax.nn.logsumexp(similarity_table, axis=1) - picked
        per_crop = live * ce
        return (loss_scale * jnp.sum(per_crop), (join_crops(after_two), per_crop))
    weights = (wa1, wb1, se_down1, se_bias1, se_up1, se_gate_bias1, wc1, wp1, scales1, shifts1, wa2, wb2, se_down2, se_bias2, se_up2, se_gate_bias2, wc2, scales2, shifts2)
    weight_values = [weight.astype(jnp.float32) for weight in weights]
    value, pullback, extra = jax.vjp(objective, pixels.astype(jnp.float32), *weight_values, has_aux=True)
    grads = pullback(jnp.float32(1.0))
    out_field, crop_loss = extra
    return (out_field.astype(jnp.bfloat16), crop_loss, grads[0].astype(jnp.bfloat16), grads[1], grads[2], grads[3], grads[4], grads[5], grads[6], grads[7], grads[8], grads[9], grads[10], grads[11], grads[12], grads[13], grads[14], grads[15], grads[16], grads[17], grads[18], grads[19])
```

```python
import functools

import jax
import jax.numpy as jnp
import numpy as np
from jax import lax
from jax.experimental import pallas as pl
from jax.experimental.pallas import tpu as pltpu
from jax.sharding import PartitionSpec as P

GW = 56
COUNTS = (5, 3, 2)
SIDES_IN = (10, 14, 18)
SIDES_OUT = (5, 7, 9)
CROPS = sum(COUNTS)
ROWS = sum(n * s * s for n, s in zip(COUNTS, SIDES_OUT))
ROWS_IN = sum(n * s * s for n, s in zip(COUNTS, SIDES_IN))
R = -(-ROWS // 64) * 64
SLOTS = 16
LOSS_SCALE = 256.0
SHARPNESS = 0.1
BF = jnp.bfloat16
F32 = jnp.float32
MESH = pl.DeviceIdType.MESH
VMEM_LIMIT = 60 * 1024 * 1024
PHASES = ((0, 0), (0, 1), (1, 0), (1, 1))
NCH = 4


def pixel_order():
    src = np.full((4, R), -1, np.int32)
    for phase, (pr, pc) in enumerate(PHASES):
        row, base = 0, 0
        for count, side in zip(COUNTS, SIDES_IN):
            half = side // 2
            for crop in range(count):
                for i in range(half):
                    for j in range(half):
                        src[phase, row] = base + (2 * i + pr) * side + 2 * j + pc
                        row += 1
                base += side * side
    return src.reshape(-1)


def shift_tables():
    tables = np.zeros((9, R, R), np.float32)
    row = 0
    for count, side in zip(COUNTS, SIDES_OUT):
        for crop in range(count):
            for i in range(side):
                for j in range(side):
                    for di in (-1, 0, 1):
                        for dj in (-1, 0, 1):
                            if 0 <= i + di < side and 0 <= j + dj < side:
                                tables[3 * (di + 1) + dj + 1, row, row + di * side + dj] = 1.0
                    row += 1
    return tables


def crop_tables():
    spread = np.zeros((R, SLOTS), np.float32)
    inverse = np.zeros((SLOTS, 128), np.float32)
    row, slot = 0, 0
    for count, side in zip(COUNTS, SIDES_OUT):
        for crop in range(count):
            spread[row : row + side * side, slot] = 1.0
            inverse[slot] = 1.0 / (side * side)
            row += side * side
            slot += 1
    return spread, inverse


def dot(a, b):
    return jnp.dot(a, b, preferred_element_type=F32)


def dot_nt(a, b):
    return lax.dot_general(a, b, (((1,), (1,)), ((), ())), preferred_element_type=F32)


def dot_tn(a, b):
    return lax.dot_general(a, b, (((0,), (0,)), ((), ())), preferred_element_type=F32)


def halves(v):
    high = v.astype(BF)
    return high, (v - high.astype(F32)).astype(BF)


def dot2(v, w):
    high, low = halves(v)
    return dot(high, w) + dot(low, w)


def dot2_nt(v, w):
    high, low = halves(v)
    return dot_nt(high, w) + dot_nt(low, w)


def spread_rows(table, v):
    high, low = halves(v)
    return dot(table, high) + dot(table, low)


def silu(v):
    return v * jax.nn.sigmoid(v)


def silu_slope(v):
    sig = jax.nn.sigmoid(v)
    return sig * (1.0 + v * (1.0 - sig))


STEP = 32


def by_rows(body, init=0, rows=R, step=STEP):
    def one(i, carry):
        return body(pl.ds(pl.multiple_of(i * step, step), step), carry)

    return lax.fori_loop(0, rows // step, one, init)


def colsum(v):
    return jnp.sum(v, axis=0, keepdims=True)


class Link:
    def __init__(self, send, recv):
        self.send, self.recv, self.used = send, recv, 0
        self.flying = []

    def to(self, src, dst, peer):
        copy = pltpu.make_async_remote_copy(
            src_ref=src,
            dst_ref=dst,
            send_sem=self.send.at[self.used],
            recv_sem=self.recv.at[self.used],
            device_id={"chan": peer},
            device_id_type=MESH,
        )
        self.used += 1
        copy.start()
        self.flying.append(copy)
        return copy

    def finish(self):
        for copy in self.flying:
            copy.wait_send()
        self.flying = []


def greet(me):
    barrier = pltpu.get_barrier_semaphore()
    for other in (1, 2, 3):
        pl.semaphore_signal(
            barrier, inc=1, device_id={"chan": me ^ other}, device_id_type=MESH
        )
    pl.semaphore_wait(barrier, 3)


PIECES = 2
PIECE = R // PIECES


def piece(h):
    return pl.ds(h * PIECE, PIECE)


def gather_chunks(link, me, box):
    across = [link.to(box.at[me, piece(h)], box.at[me, piece(h)], me ^ 2) for h in range(PIECES)]
    beside = [link.to(box.at[me, piece(h)], box.at[me, piece(h)], me ^ 1) for h in range(PIECES)]
    passed = []
    for h in range(PIECES):
        across[h].wait_recv()
        passed.append(link.to(box.at[me ^ 2, piece(h)], box.at[me ^ 2, piece(h)], me ^ 1))
    for h in range(PIECES):
        beside[h].wait_recv()
        passed[h].wait_recv()


def sum_small(link, me, box):
    return [link.to(box.at[me], box.at[me], me ^ other) for other in (1, 2, 3)]


def scatter_start(link, me, parts, from_core, h):
    first = link.to(parts.at[me ^ 3, piece(h)], from_core.at[0, piece(h)], me ^ 1)
    second = link.to(parts.at[me ^ 1, piece(h)], from_core.at[1, piece(h)], me ^ 1)
    return first, second


def scatter_pass(link, me, parts, from_core, from_y, h, started):
    started[0].wait_recv()

    def add(i, carry):
        rows = pl.ds(pl.multiple_of(h * PIECE + i * STEP, STEP), STEP)
        parts[me ^ 2, rows] = (
            parts[me ^ 2, rows].astype(F32) + from_core[0, rows].astype(F32)
        ).astype(BF)
        return carry

    lax.fori_loop(0, PIECE // STEP, add, 0)
    return link.to(parts.at[me ^ 2, piece(h)], from_y.at[piece(h)], me ^ 2)


def conv_forward(taps, act, kernel, shifts, grouped):
    for tap, phase, move in taps:
        if move is None:
            moved = act[phase]
        else:
            moved = dot(shifts[move], act[phase]).astype(BF)
        grouped[...] += dot(moved, kernel[tap])


def pool(crop_rows, inverse, field, high, low):
    def split(rows, carry):
        a, b = halves(field[rows])
        high[rows] = a
        low[rows] = b
        return carry

    by_rows(split)
    return (dot(crop_rows[...], high[...]) + dot(crop_rows[...], low[...])) * inverse[:, :1]


def excite(link, me, k, s):
    gains, shifts = k["gains"], k["moves"]

    def activate(rows, carry):
        s["grouped_act"][rows] = silu(gains[1:2] * k["grouped"][rows] + shifts[1:2])
        return carry

    by_rows(activate)
    pooled = pool(k["crop_rows"], k["inverse"], s["grouped_act"], s["high"], s["low"])
    k["pooled"][...] = pooled
    s["hidden_box"][me] = dot2(pooled, k["down"][...])
    terms = sum_small(link, me, s["hidden_box"])
    yield
    for term in terms:
        term.wait_recv()
    box = s["hidden_box"]
    hidden_pre = box[0] + box[1] + box[2] + box[3] + k["down_bias"][...]
    k["hidden_pre"][...] = hidden_pre
    gating = jax.nn.sigmoid(dot2(silu(hidden_pre), k["up"][...]) + k["up_bias"][...])
    k["gating"][...] = gating
    s["wide"][...] = spread_rows(k["spread"][...], gating)

    def scale(rows, carry):
        k["excited"][rows] = (s["grouped_act"][rows] * s["wide"][rows]).astype(BF)
        return carry

    by_rows(scale)


def scatter_product(link, me, left, weight, parts, from_core, from_y, wide):
    started, passing = [], []
    for h in range(PIECES):
        for chunk in range(NCH):
            parts[chunk, piece(h)] = dot(left[piece(h)], weight[chunk]).astype(BF)
        started.append(scatter_start(link, me, parts, from_core, h))
    for h in range(PIECES):
        passing.append(scatter_pass(link, me, parts, from_core, from_y, h, started[h]))
    return started, passing


def scatter_product_nt(link, me, left, weight, parts, from_core, from_y):
    started, passing = [], []
    for h in range(PIECES):
        for chunk in range(NCH):
            parts[chunk, piece(h)] = dot_nt(left[piece(h)], weight[chunk]).astype(BF)
        started.append(scatter_start(link, me, parts, from_core, h))
    for h in range(PIECES):
        passing.append(scatter_pass(link, me, parts, from_core, from_y, h, started[h]))
    return started, passing


def scatter_end(started, passing):
    for first, second in started:
        second.wait_recv()
    for copy in passing:
        copy.wait_recv()


STRIDED_TAPS = {
    3: ((0, 3, 0), (2, 3, 1), (6, 3, 2), (8, 3, None)),
    2: ((1, 2, 1), (7, 2, None)),
    1: ((3, 1, 2), (5, 1, None)),
    0: ((4, 0, None),),
}
STRIDED_MOVES = (0, 1, 3)


def forward_one(
    own_hbm, across_hbm, wa, wp, wc, kernel, down, up, gains, moves, down_bias, up_bias,
    shift_mats, spread, crop_rows, inverse,
    box, first, act, grouped, branch, short, y1, pooled, hidden_pre, gating,
    grouped_act, high, low, wide, excited, parts, from_core, from_y, hidden_box,
    send, recv, local,
):
    me = lax.axis_index("chan")
    greet(me)
    link = Link(send, recv)
    copies, beside, passed = [], [], []
    order = (3, 2, 1, 0)
    for p in order:
        mine = pltpu.make_async_copy(own_hbm.at[p], box.at[me, p], local.at[p])
        mine.start()
        theirs = pltpu.make_async_copy(across_hbm.at[p], box.at[me ^ 2, p], local.at[4 + p])
        theirs.start()
        copies.append((mine, theirs))
        beside.append(link.to(own_hbm.at[p], box.at[me, p], me ^ 1))
        passed.append(link.to(across_hbm.at[p], box.at[me ^ 2, p], me ^ 1))
    grouped[...] = jnp.zeros(grouped.shape, F32)
    for at, p in enumerate(order):
        copies[at][0].wait()
        copies[at][1].wait()
        beside[at].wait_recv()
        passed[at].wait_recv()
        total = dot(box[0, p], wa[0])
        for chunk in range(1, NCH):
            total += dot(box[chunk, p], wa[chunk])
        first[p] = total

        def activate(rows, carry):
            act[p, rows] = silu(gains[0:1] * first[p, rows] + moves[0:1]).astype(BF)
            return carry

        by_rows(activate)
        conv_forward(STRIDED_TAPS[p], act, kernel, shift_mats, grouped)
    k = dict(
        gains=gains, moves=moves, grouped=grouped, crop_rows=crop_rows, inverse=inverse,
        pooled=pooled, down=down, up=up, down_bias=down_bias, up_bias=up_bias,
        hidden_pre=hidden_pre, gating=gating, spread=spread, excited=excited,
    )
    s = dict(grouped_act=grouped_act, high=high, low=low, hidden_box=hidden_box, wide=wide)
    steps = excite(link, me, k, s)
    next(steps)
    total = dot(box[0, 0], wp[0])
    for chunk in range(1, NCH):
        total += dot(box[chunk, 0], wp[chunk])
    short[...] = total
    next(steps, None)
    started, passing = scatter_product(link, me, excited, wc, parts, from_core, from_y, wide)
    scatter_end(started, passing)

    def leave(rows, carry):
        total = (
            parts[me, rows].astype(F32) + from_core[1, rows].astype(F32)
        ) + from_y[rows].astype(F32)
        branch[rows] = total
        preact = gains[2:3] * total + moves[2:3] + gains[3:4] * short[rows] + moves[3:4]
        y1[rows] = silu(preact).astype(BF)
        return carry

    by_rows(leave)
    link.finish()


UNIT_TAPS = tuple((tap, 0, tap) for tap in range(9))


def forward_two(
    y1, wa, wc, kernel, down, up, gains, moves, down_bias, up_bias, protos, live, target,
    shift_mats, spread, crop_rows, inverse,
    box, first, act, grouped, branch, pooled, hidden_pre, gating, block_out, loss, dm, dbranch, vector,
    grouped_act, high, low, wide, excited, parts, from_core, from_y, hidden_box,
    score_box, square_box, send, recv,
):
    me = lax.axis_index("chan")
    box[me] = y1[...]
    greet(me)
    link = Link(send, recv)
    gather_chunks(link, me, box)
    total = dot(box[0], wa[0])
    for chunk in range(1, NCH):
        total += dot(box[chunk], wa[chunk])
    first[...] = total
    grouped[...] = jnp.zeros(grouped.shape, F32)

    def activate(rows, carry):
        act[0, rows] = silu(gains[0:1] * first[rows] + moves[0:1]).astype(BF)
        return carry

    by_rows(activate)

    def one_tap(tap, carry):
        moved = dot(shift_mats[tap], act[0]).astype(BF)
        grouped[...] += dot(moved, kernel[tap])
        return carry

    lax.fori_loop(0, 9, one_tap, 0)
    k = dict(
        gains=gains, moves=moves, grouped=grouped, crop_rows=crop_rows, inverse=inverse,
        pooled=pooled, down=down, up=up, down_bias=down_bias, up_bias=up_bias,
        hidden_pre=hidden_pre, gating=gating, spread=spread, excited=excited,
    )
    s = dict(grouped_act=grouped_act, high=high, low=low, hidden_box=hidden_box, wide=wide)
    steps = excite(link, me, k, s)
    next(steps)
    next(steps, None)
    started, passing = scatter_product(link, me, excited, wc, parts, from_core, from_y, wide)
    scatter_end(started, passing)

    def leave(rows, carry):
        total = (
            parts[me, rows].astype(F32) + from_core[1, rows].astype(F32)
        ) + from_y[rows].astype(F32)
        branch[rows] = total
        preact = gains[2:3] * total + moves[2:3] + y1[rows].astype(F32)
        wide[rows] = preact
        y2 = silu(preact)
        grouped_act[rows] = y2
        block_out[rows] = y2.astype(BF)
        return carry

    by_rows(leave)
    emb = pool(crop_rows, inverse, grouped_act, high, low)
    score_box[me] = dot2(emb, protos[...]).astype(BF)
    square_box[me] = jnp.broadcast_to(
        jnp.sum(emb * emb, axis=1, keepdims=True), square_box.shape[1:]
    )
    terms = sum_small(link, me, score_box) + sum_small(link, me, square_box)
    for term in terms:
        term.wait_recv()
    raw = (score_box[0].astype(F32) + score_box[1].astype(F32)) + (
        score_box[2].astype(F32) + score_box[3].astype(F32)
    )
    squares = (square_box[0] + square_box[1] + square_box[2] + square_box[3])[:, :1]
    inv_norm = lax.rsqrt(squares + 1e-6)
    inv_scale = inv_norm * (1.0 / SHARPNESS)
    scores = raw * inv_scale
    onehot = (
        lax.broadcasted_iota(jnp.int32, scores.shape, 1) == target[:, :1]
    ).astype(F32)
    top = jnp.max(scores, axis=1, keepdims=True)
    powers = jnp.exp(scores - top)
    mass = jnp.sum(powers, axis=1, keepdims=True)
    entropy = top + jnp.log(mass) - jnp.sum(onehot * scores, axis=1, keepdims=True)
    alive = live[:, :1]
    loss[...] = jnp.broadcast_to(alive * entropy, loss.shape)
    dscores = LOSS_SCALE * alive * (powers / mass - onehot)
    along = jnp.sum(dscores * scores, axis=1, keepdims=True)
    demb = dot2_nt(dscores, protos[...]) * inv_scale - along * inv_norm * inv_norm * emb
    high[...] = dot2_rows(spread, demb * inverse[:, :1], dm)

    def back(rows, carry):
        masked = dm[rows] * silu_slope(wide[rows])
        dm[rows] = masked
        dbranch[rows] = (gains[2:3] * masked).astype(BF)
        return carry[0] + colsum(masked * branch[rows]), carry[1] + colsum(masked)

    zero = jnp.zeros((1, dm.shape[1]), F32)
    gain_grad, shift_grad = by_rows(back, (zero, zero))
    vector[0:1] = gain_grad
    vector[1:2] = shift_grad
    link.finish()


def dot2_rows(spread, v, out):
    out[...] = spread_rows(spread[...], v)
    return jnp.zeros(out.shape, BF)


def fold_groups(full, columns_group):
    total = jnp.zeros((GW, full.shape[1]), F32)
    for group in range(full.shape[0] // GW):
        total = total + jnp.where(
            columns_group == group, full[group * GW : (group + 1) * GW], 0.0
        )
    return total


def backward(
    strided,
    box_in, dbranch_in, dm_in, dshort_in, wa, wp, wc, kernel, down, up, gains, moves, first, act, grouped,
    hidden_pre, gating, shift_mats, spread, crop_rows, inverse,
    grad_wa, grad_wp, grad_wc, grad_kernel, dz, dhidden, vector, dx,
    dbox, dexcited, grouped_act, high, low, wide, excited, dgrouped, dact, dfirst, hidden_box,
    parts, from_core, from_y, chunks, local, send, recv,
):
    phases = 4 if strided else 1
    me = lax.axis_index("chan")
    loads = [
        pltpu.make_async_copy(box_in.at[chunk], chunks.at[chunk % 2], local.at[chunk])
        for chunk in range(NCH)
    ]
    loads[0].start()
    loads[1].start()
    dbox[me] = dbranch_in[...]
    greet(me)
    link = Link(send, recv)
    gather_chunks(link, me, dbox)
    total = dot_nt(dbox[0], wc[0])
    for chunk in range(1, NCH):
        total += dot_nt(dbox[chunk], wc[chunk])
    dexcited[...] = total
    wide[...] = spread_rows(spread[...], gating[...])

    def gate(rows, carry):
        value = silu(gains[1:2] * grouped[rows] + moves[1:2])
        excited[rows] = (value * wide[rows]).astype(BF)
        grouped_act[rows] = dexcited[rows] * value
        return carry

    by_rows(gate)
    ones = jnp.ones((SLOTS, 128), F32)
    dgating = pool(crop_rows, ones, grouped_act, high, low)
    gates = gating[...]
    gate_pre = dgating * gates * (1.0 - gates)
    dz[...] = gate_pre
    hidden_box[me] = dot2_nt(gate_pre, up[...])
    terms = sum_small(link, me, hidden_box)

    def grad_last(chunk, carry):
        grad_wc[chunk] = dot_tn(excited[...], dbox[chunk]).astype(BF)
        return carry

    lax.fori_loop(0, NCH, grad_last, 0)
    for term in terms:
        term.wait_recv()
    hidden_grad = (hidden_box[0] + hidden_box[1] + hidden_box[2] + hidden_box[3]) * silu_slope(
        hidden_pre[...]
    )
    dhidden[...] = hidden_grad
    dpooled = dot2_nt(hidden_grad, down[...]) * inverse[:, :1]
    grouped_act[...] = spread_rows(spread[...], dpooled)

    def through(rows, carry):
        value = grouped[rows]
        grad = (dexcited[rows] * wide[rows] + grouped_act[rows]) * silu_slope(
            gains[1:2] * value + moves[1:2]
        )
        dgrouped[rows] = (gains[1:2] * grad).astype(BF)
        return carry[0] + colsum(grad * value), carry[1] + colsum(grad)

    zero = jnp.zeros((1, wide.shape[1]), F32)
    gain_mid, shift_mid = by_rows(through, (zero, zero))
    vector[0:1] = jnp.sum(gate_pre, axis=0, keepdims=True)
    vector[1:2] = jnp.sum(hidden_grad, axis=0, keepdims=True)
    vector[2:3] = gain_mid
    vector[3:4] = shift_mid
    columns_group = lax.broadcasted_iota(jnp.int32, (GW, wide.shape[1]), 1) // GW
    for p in range(phases):
        dact[p] = jnp.zeros(dact.shape[1:], F32)
    if strided:
        for p in range(phases):
            for tap, phase, move in STRIDED_TAPS[p]:
                if move is None:
                    back = dgrouped[...]
                else:
                    back = dot(shift_mats[move], dgrouped[...]).astype(BF)
                dact[phase] += dot_nt(back, kernel[tap])
                grad_kernel[tap] = fold_groups(dot_tn(act[phase], back), columns_group)
    else:

        def one_tap(tap, carry):
            back = dot(shift_mats[8 - tap], dgrouped[...]).astype(BF)
            dact[0] += dot_nt(back, kernel[tap])
            grad_kernel[tap] = fold_groups(dot_tn(act[0], back), columns_group)
            return carry

        lax.fori_loop(0, 9, one_tap, 0)
    sums = (zero, zero)
    for p in range(phases):

        def enter(rows, carry):
            value = first[p, rows]
            grad = dact[p, rows] * silu_slope(gains[0:1] * value + moves[0:1])
            dfirst[p, rows] = (gains[0:1] * grad).astype(BF)
            return carry[0] + colsum(grad * value), carry[1] + colsum(grad)

        sums = by_rows(enter, sums)
    vector[4:5] = sums[0]
    vector[5:6] = sums[1]
    waits = []
    for p in range(phases):
        started, passing = [], []
        mine, core, far = parts.at[p], from_core.at[p], from_y.at[p]
        for h in range(PIECES):
            for chunk in range(NCH):
                total = dot_nt(dfirst[p, piece(h)], wa[chunk])
                if strided and p == 0:
                    total += dot_nt(dshort_in[piece(h)], wp[chunk])
                mine[chunk, piece(h)] = total.astype(BF)
            started.append(scatter_start(link, me, mine, core, h))
        for h in range(PIECES):
            passing.append(scatter_pass(link, me, mine, core, far, h, started[h]))
        waits.append((started, passing))
    for chunk in range(NCH):
        loads[chunk].wait()
        held = chunks.at[chunk % 2]
        total = dot_tn(held[0], dfirst[0])
        for p in range(1, phases):
            total += dot_tn(held[p], dfirst[p])
        grad_wa[chunk] = total.astype(BF)
        if strided:
            grad_wp[chunk] = dot_tn(held[0], dshort_in[...]).astype(BF)
        if chunk + 2 < NCH:
            loads[chunk + 2].start()
    for started, passing in waits:
        scatter_end(started, passing)
    for p in range(phases):

        def leave(rows, carry):
            total = (
                parts[p, me, rows].astype(F32) + from_core[p, 1, rows].astype(F32)
            ) + from_y[p, rows].astype(F32)
            if not strided:
                total = total + dm_in[rows]
            dx[p, rows] = total.astype(dx.dtype)
            return carry

        by_rows(leave)
    link.finish()


def enter_one(dy, branch, short, gains, moves, dbranch, dshort, vector):
    def body(rows, carry):
        preact = (
            gains[2:3] * branch[rows] + moves[2:3] + gains[3:4] * short[rows] + moves[3:4]
        )
        masked = dy[0, rows] * silu_slope(preact)
        dbranch[rows] = (gains[2:3] * masked).astype(BF)
        dshort[rows] = (gains[3:4] * masked).astype(BF)
        return (
            carry[0] + colsum(masked * branch[rows]),
            carry[1] + colsum(masked * short[rows]),
            carry[2] + colsum(masked),
        )

    zero = jnp.zeros((1, branch.shape[1]), F32)
    sums = by_rows(body, (zero, zero, zero))
    vector[0:1] = sums[0]
    vector[1:2] = sums[1]
    vector[2:3] = sums[2]


def vm():
    return pl.BlockSpec(memory_space=pltpu.VMEM)


def shape(dims, dtype=F32):
    return jax.ShapeDtypeStruct(dims, dtype)


def params(number):
    if number is None:
        return pltpu.CompilerParams(vmem_limit_bytes=VMEM_LIMIT)
    return pltpu.CompilerParams(
        vmem_limit_bytes=VMEM_LIMIT, collective_id=number, has_side_effects=True
    )


def call(kernel, number, ins, specs, outs, scratch):
    return pl.pallas_call(
        kernel,
        out_shape=outs,
        in_specs=specs,
        out_specs=[vm()] * len(outs),
        scratch_shapes=scratch,
        compiler_params=params(number),
    )(*ins)


def sems(n):
    return pltpu.SemaphoreType.DMA((n,))


def small(rows, width, dtype):
    return pltpu.VMEM((rows, width), dtype)


def dense_kernel(kernel):
    width = kernel.shape[-1]
    groups = width // GW
    tiled = jnp.tile(kernel, (1, groups, 1))
    row = lax.broadcasted_iota(jnp.int32, (width, width), 0) // GW
    col = lax.broadcasted_iota(jnp.int32, (width, width), 1) // GW
    return jnp.where((row == col)[None], tiled, jnp.zeros((), kernel.dtype))


def per_device(
    pixels, wa1, wb1, se_down1, se_bias1, se_up1, se_gate_bias1, wc1, wp1, scales1, shifts1,
    wa2, wb2, se_down2, se_bias2, se_up2, se_gate_bias2, wc2, scales2, shifts2,
    prototypes, live_counts, crop_image, codes,
):
    C = pixels.shape[1]
    D = wa1.shape[0]
    order = pixel_order()
    spread_np, inverse_np = crop_tables()
    tables_np = shift_tables()
    shift_mats = jnp.asarray(tables_np, BF)
    ahead = jnp.asarray(tables_np[[m for m in STRIDED_MOVES]], BF)
    behind = jnp.asarray(tables_np[[8 - m for m in STRIDED_MOVES]], BF)
    spread = jnp.asarray(spread_np, BF)
    crop_rows = jnp.asarray(spread_np.T.copy(), BF)
    inverse = jnp.asarray(inverse_np, F32)
    place = jnp.asarray(order)[:, None] == jnp.arange(ROWS_IN, dtype=jnp.int32)[None, :]
    place = place.astype(BF)
    own = jnp.dot(place, pixels, preferred_element_type=F32).astype(BF).reshape(4, R, C)
    across = lax.ppermute(own, "chan", [(c, c ^ 2) for c in range(NCH)])
    rows4 = lambda w: w.reshape(NCH, C, C)
    cols4 = lambda w: w.reshape(C, NCH, C).transpose(1, 0, 2)
    line = lambda v: v.reshape(1, -1)
    wa1r, wp1r, wa2r = rows4(wa1), rows4(wp1), rows4(wa2)
    wc1r, wc2r = cols4(wc1), cols4(wc2)
    kernel1, kernel2 = dense_kernel(wb1), dense_kernel(wb2)
    bias = [line(v) for v in (se_bias1, se_gate_bias1, se_bias2, se_gate_bias2)]
    field = small(R, C, F32)
    low = small(R, C, BF)
    comm = [
        pltpu.VMEM((NCH, R, C), BF),
        pltpu.VMEM((2, R, C), BF),
        low,
        pltpu.VMEM((NCH, SLOTS, C), F32),
    ]
    any_ = pl.BlockSpec(memory_space=pl.ANY)
    ins = (
        own, across, wa1r, wp1r, wc1r, kernel1, se_down1, se_up1, scales1, shifts1, bias[0], bias[1],
        ahead, spread, crop_rows, inverse,
    )
    box1, first1, act1, grouped1, branch1, short1, y1, pooled1, hidden_pre1, gating1 = call(
        forward_one, 0, ins, [any_] * 2 + [vm()] * 14,
        [
            shape((NCH, 4, R, C), BF), shape((4, R, C)), shape((4, R, C), BF), shape((R, C)),
            shape((R, C)), shape((R, C)), shape((R, C), BF), shape((SLOTS, C)), shape((SLOTS, C)),
            shape((SLOTS, C)),
        ],
        [field, low, low, field, low] + comm + [sems(24), sems(24), sems(8)],
    )
    lives = jnp.concatenate(
        [
            (jnp.arange(count, dtype=jnp.int32) < live_counts[bucket]).astype(F32)
            for bucket, count in enumerate(COUNTS)
        ]
        + [jnp.zeros((SLOTS - CROPS,), F32)]
    )
    match = crop_image[:, None] == jnp.arange(codes.shape[0], dtype=jnp.int32)[None, :]
    target = jnp.pad(jnp.sum(jnp.where(match, codes[None, :], 0), axis=1), (0, SLOTS - CROPS))
    lives = jnp.broadcast_to(lives[:, None], (SLOTS, 128))
    target = jnp.broadcast_to(target[:, None], (SLOTS, 128)).astype(jnp.int32)
    protos = prototypes.shape[1]
    ins = (
        y1, wa2r, wc2r, kernel2, se_down2, se_up2, scales2, shifts2, bias[2], bias[3], prototypes,
        lives, target, shift_mats, spread, crop_rows, inverse,
    )
    (
        box2, first2, act2, grouped2, branch2, pooled2, hidden_pre2, gating2, block_out, loss, dm2, dbranch2,
        vector2,
    ) = call(
        forward_two, 1, ins, [vm()] * 17,
        [
            shape((NCH, R, C), BF), shape((R, C)), shape((1, R, C), BF), shape((R, C)), shape((R, C)),
            shape((SLOTS, C)), shape((SLOTS, C)), shape((SLOTS, C)), shape((R, C), BF),
            shape((SLOTS, 128)), shape((R, C)), shape((R, C), BF), shape((8, C)),
        ],
        [field, low, low, field, low] + comm
        + [
            pltpu.VMEM((NCH, SLOTS, protos), BF), pltpu.VMEM((NCH, SLOTS, 128), F32),
            sems(32), sems(32),
        ],
    )
    hidden_box = pltpu.VMEM((NCH, SLOTS, C), F32)

    def back(number, strided, ins):
        n = 4 if strided else 1
        outs = [
            shape((NCH, C, C), BF),
            shape((NCH, C, C), BF) if strided else shape((8, 128), BF),
            shape((NCH, C, C), BF), shape((9, GW, C)), shape((SLOTS, C)), shape((SLOTS, C)),
            shape((8, C)), shape((n, R, C), BF if strided else F32),
        ]
        scratch = [
            pltpu.VMEM((NCH, R, C), BF), field, field, low, low, field, low, low,
            pltpu.VMEM((n, R, C), F32), pltpu.VMEM((n, R, C), BF), hidden_box,
            pltpu.VMEM((n, NCH, R, C), BF), pltpu.VMEM((n, 2, R, C), BF), pltpu.VMEM((n, R, C), BF),
            pltpu.VMEM((2, n, R, C), BF), sems(NCH), sems(40), sems(40),
        ]
        return call(
            functools.partial(backward, strided), number, ins, [any_] + [vm()] * (len(ins) - 1), outs, scratch
        )

    tables = (shift_mats, spread, crop_rows, inverse)
    grad_wa2, _, grad_wc2, grad_wb2, dz2, dhidden2, vec2, dy1 = back(
        2, False,
        (
            box2[:, None], dbranch2, dm2, vector2, wa2r, vector2, wc2r, kernel2, se_down2, se_up2, scales2,
            shifts2, first2[None], act2, grouped2, hidden_pre2, gating2,
        )
        + tables,
    )
    dbranch1, dshort1, vector1 = call(
        enter_one, None, (dy1, branch1, short1, scales1, shifts1), [vm()] * 5,
        [shape((R, C), BF), shape((R, C), BF), shape((8, C))], [],
    )
    grad_wa1, grad_wp1, grad_wc1, grad_wb1, dz1, dhidden1, vec1, dx = back(
        3, True,
        (
            box1, dbranch1, vec2, dshort1, wa1r, wp1r, wc1r, kernel1, se_down1, se_up1, scales1,
            shifts1, first1, act1, grouped1, hidden_pre1, gating1, behind, spread, crop_rows, inverse,
        ),
    )
    flat_dx = dx.reshape(4 * R, C)
    pixels_grad = lax.dot_general(
        place, flat_dx, (((0,), (0,)), ((), ())), preferred_element_type=F32
    ).astype(BF)
    exact = lambda a, b: lax.dot_general(
        a, b, (((0,), (0,)), ((), ())), precision=lax.Precision.HIGHEST
    ).astype(BF)
    hidden1, hidden2 = silu(hidden_pre1), silu(hidden_pre2)
    se = [
        exact(pooled1, dhidden1), exact(hidden1, dz1), exact(pooled2, dhidden2), exact(hidden2, dz2),
    ]
    gain1 = jnp.stack([vec1[4], vec1[2], vector1[0], vector1[1]])
    shift1 = jnp.stack([vec1[5], vec1[3], vector1[2], vector1[2]])
    gain2 = jnp.stack([vec2[4], vec2[2], vector2[0]])
    shift2 = jnp.stack([vec2[5], vec2[3], vector2[1]])
    vectors = jnp.concatenate([gain1, shift1, gain2, shift2, vec1[:2], vec2[:2]]).astype(BF)
    summed = lax.psum(
        (
            grad_wa1, grad_wp1, grad_wc1, grad_wb1.astype(BF), grad_wa2, grad_wc2, grad_wb2.astype(BF),
            *se, vectors,
        ),
        "dp",
    )
    wide = [v.astype(F32) for v in summed]
    from_rows = lambda w: w.reshape(D, C)
    from_cols = lambda w: w.transpose(1, 0, 2).reshape(C, NCH * C)
    v = wide[11]
    return (
        block_out[:ROWS],
        loss[:CROPS, 0],
        pixels_grad,
        from_rows(wide[0]),
        wide[3],
        wide[7],
        v[15],
        wide[8],
        v[14],
        from_cols(wide[2]),
        from_rows(wide[1]),
        v[0:4],
        v[4:8],
        from_rows(wide[4]),
        wide[6],
        wide[9],
        v[17],
        wide[10],
        v[16],
        from_cols(wide[5]),
        v[8:11],
        v[11:14],
    )


def solution(mesh):
    col, row, deep, whole = P(None, "chan"), P("chan", None), P(None, None, "chan"), P()
    one = (col, deep, row, whole, col, P("chan"), row, col, col, col)
    two = (col, deep, row, whole, col, P("chan"), row, col, col)
    return jax.shard_map(
        per_device,
        mesh=mesh,
        in_specs=(P("dp", "chan"), *one, *two, row, P("dp"), P("dp"), P("dp")),
        out_specs=(P("dp", "chan"), P("dp"), P("dp", "chan"), *one, *two),
        check_vma=False,
    )
```

```python
import functools

import jax
import jax.numpy as jnp
import numpy as np
from jax import lax
from jax.experimental import pallas as pl
from jax.experimental.pallas import tpu as pltpu
from jax.sharding import PartitionSpec as P

GW = 56
COUNTS = (5, 3, 2)
SIDES_IN = (10, 14, 18)
SIDES_OUT = (5, 7, 9)
CROPS = sum(COUNTS)
ROWS = sum(n * s * s for n, s in zip(COUNTS, SIDES_OUT))
ROWS_IN = sum(n * s * s for n, s in zip(COUNTS, SIDES_IN))
R = -(-ROWS // 64) * 64
SLOTS = 16
LOSS_SCALE = 256.0
SHARPNESS = 0.1
BF = jnp.bfloat16
F32 = jnp.float32
MESH = pl.DeviceIdType.MESH
VMEM_LIMIT = 60 * 1024 * 1024
PHASES = ((0, 0), (0, 1), (1, 0), (1, 1))
NCH = 4


def pixel_order():
    src = np.full((4, R), -1, np.int32)
    for phase, (pr, pc) in enumerate(PHASES):
        row, base = 0, 0
        for count, side in zip(COUNTS, SIDES_IN):
            half = side // 2
            for crop in range(count):
                for i in range(half):
                    for j in range(half):
                        src[phase, row] = base + (2 * i + pr) * side + 2 * j + pc
                        row += 1
                base += side * side
    return src.reshape(-1)


def shift_tables():
    tables = np.zeros((9, R, R), np.float32)
    row = 0
    for count, side in zip(COUNTS, SIDES_OUT):
        for crop in range(count):
            for i in range(side):
                for j in range(side):
                    for di in (-1, 0, 1):
                        for dj in (-1, 0, 1):
                            if 0 <= i + di < side and 0 <= j + dj < side:
                                tables[3 * (di + 1) + dj + 1, row, row + di * side + dj] = 1.0
                    row += 1
    return tables


def crop_tables():
    spread = np.zeros((R, SLOTS), np.float32)
    inverse = np.zeros((SLOTS, 128), np.float32)
    row, slot = 0, 0
    for count, side in zip(COUNTS, SIDES_OUT):
        for crop in range(count):
            spread[row : row + side * side, slot] = 1.0
            inverse[slot] = 1.0 / (side * side)
            row += side * side
            slot += 1
    return spread, inverse


def dot(a, b):
    return jnp.dot(a, b, preferred_element_type=F32)


def dot_nt(a, b):
    return lax.dot_general(a, b, (((1,), (1,)), ((), ())), preferred_element_type=F32)


def dot_tn(a, b):
    return lax.dot_general(a, b, (((0,), (0,)), ((), ())), preferred_element_type=F32)


def halves(v):
    high = v.astype(BF)
    return high, (v - high.astype(F32)).astype(BF)


def dot2(v, w):
    high, low = halves(v)
    return dot(high, w) + dot(low, w)


def dot2_nt(v, w):
    high, low = halves(v)
    return dot_nt(high, w) + dot_nt(low, w)


def spread_rows(table, v):
    high, low = halves(v)
    return dot(table, high) + dot(table, low)


def silu(v):
    return v * jax.nn.sigmoid(v)


def silu_slope(v):
    sig = jax.nn.sigmoid(v)
    return sig * (1.0 + v * (1.0 - sig))


STEP = 32


def by_rows(body, init=0, rows=R, step=STEP):
    def one(i, carry):
        return body(pl.ds(pl.multiple_of(i * step, step), step), carry)

    return lax.fori_loop(0, rows // step, one, init)


def colsum(v):
    return jnp.sum(v, axis=0, keepdims=True)


class Link:
    def __init__(self, send, recv):
        self.send, self.recv, self.used = send, recv, 0
        self.flying = []

    def to(self, src, dst, peer):
        copy = pltpu.make_async_remote_copy(
            src_ref=src,
            dst_ref=dst,
            send_sem=self.send.at[self.used],
            recv_sem=self.recv.at[self.used],
            device_id={"chan": peer},
            device_id_type=MESH,
        )
        self.used += 1
        copy.start()
        self.flying.append(copy)
        return copy

    def finish(self):
        for copy in self.flying:
            copy.wait_send()
        self.flying = []


def greet(me):
    barrier = pltpu.get_barrier_semaphore()
    for other in (1, 2, 3):
        pl.semaphore_signal(
            barrier, inc=1, device_id={"chan": me ^ other}, device_id_type=MESH
        )
    pl.semaphore_wait(barrier, 3)


PIECES = 2
PIECE = R // PIECES


def piece(h):
    return pl.ds(h * PIECE, PIECE)


def gather_chunks(link, me, box):
    across = [link.to(box.at[me, piece(h)], box.at[me, piece(h)], me ^ 2) for h in range(PIECES)]
    beside = [link.to(box.at[me, piece(h)], box.at[me, piece(h)], me ^ 1) for h in range(PIECES)]
    passed = []
    for h in range(PIECES):
        across[h].wait_recv()
        passed.append(link.to(box.at[me ^ 2, piece(h)], box.at[me ^ 2, piece(h)], me ^ 1))
    for h in range(PIECES):
        beside[h].wait_recv()
        passed[h].wait_recv()


def sum_small(link, me, box):
    return [link.to(box.at[me], box.at[me], me ^ other) for other in (1, 2, 3)]


def scatter_start(link, me, parts, from_core, h):
    first = link.to(parts.at[me ^ 3, piece(h)], from_core.at[0, piece(h)], me ^ 1)
    second = link.to(parts.at[me ^ 1, piece(h)], from_core.at[1, piece(h)], me ^ 1)
    return first, second


def scatter_pass(link, me, parts, from_core, from_y, h, started):
    started[0].wait_recv()

    def add(i, carry):
        rows = pl.ds(pl.multiple_of(h * PIECE + i * STEP, STEP), STEP)
        parts[me ^ 2, rows] = (
            parts[me ^ 2, rows].astype(F32) + from_core[0, rows].astype(F32)
        ).astype(BF)
        return carry

    lax.fori_loop(0, PIECE // STEP, add, 0)
    return link.to(parts.at[me ^ 2, piece(h)], from_y.at[piece(h)], me ^ 2)


def conv_forward(taps, act, kernel, shifts, grouped):
    for tap, phase, move in taps:
        if move is None:
            moved = act[phase]
        else:
            moved = dot(shifts[move], act[phase]).astype(BF)
        grouped[...] += dot(moved, kernel[tap])


def pool(crop_rows, inverse, field, high, low):
    def split(rows, carry):
        a, b = halves(field[rows])
        high[rows] = a
        low[rows] = b
        return carry

    by_rows(split)
    return (dot(crop_rows[...], high[...]) + dot(crop_rows[...], low[...])) * inverse[:, :1]


def excite(link, me, k, s):
    gains, shifts = k["gains"], k["moves"]

    def activate(rows, carry):
        s["grouped_act"][rows] = silu(gains[1:2] * k["grouped"][rows] + shifts[1:2])
        return carry

    by_rows(activate)
    pooled = pool(k["crop_rows"], k["inverse"], s["grouped_act"], s["high"], s["low"])
    k["pooled"][...] = pooled
    s["hidden_box"][me] = dot2(pooled, k["down"][...])
    terms = sum_small(link, me, s["hidden_box"])
    yield
    for term in terms:
        term.wait_recv()
    box = s["hidden_box"]
    hidden_pre = box[0] + box[1] + box[2] + box[3] + k["down_bias"][...]
    k["hidden_pre"][...] = hidden_pre
    gating = jax.nn.sigmoid(dot2(silu(hidden_pre), k["up"][...]) + k["up_bias"][...])
    k["gating"][...] = gating
    s["wide"][...] = spread_rows(k["spread"][...], gating)

    def scale(rows, carry):
        k["excited"][rows] = (s["grouped_act"][rows] * s["wide"][rows]).astype(BF)
        return carry

    by_rows(scale)


def scatter_product(link, me, left, weight, parts, from_core, from_y, wide):
    started, passing = [], []
    for h in range(PIECES):
        for chunk in range(NCH):
            parts[chunk, piece(h)] = dot(left[piece(h)], weight[chunk]).astype(BF)
        started.append(scatter_start(link, me, parts, from_core, h))
    for h in range(PIECES):
        passing.append(scatter_pass(link, me, parts, from_core, from_y, h, started[h]))
    return started, passing


def scatter_product_nt(link, me, left, weight, parts, from_core, from_y):
    started, passing = [], []
    for h in range(PIECES):
        for chunk in range(NCH):
            parts[chunk, piece(h)] = dot_nt(left[piece(h)], weight[chunk]).astype(BF)
        started.append(scatter_start(link, me, parts, from_core, h))
    for h in range(PIECES):
        passing.append(scatter_pass(link, me, parts, from_core, from_y, h, started[h]))
    return started, passing


def scatter_end(started, passing):
    for first, second in started:
        second.wait_recv()
    for copy in passing:
        copy.wait_recv()


STRIDED_TAPS = {
    3: ((0, 3, 0), (2, 3, 1), (6, 3, 2), (8, 3, None)),
    2: ((1, 2, 1), (7, 2, None)),
    1: ((3, 1, 2), (5, 1, None)),
    0: ((4, 0, None),),
}
STRIDED_MOVES = (0, 1, 3)


def forward_one(
    own_hbm, across_hbm, wa, wp, wc, kernel, down, up, gains, moves, down_bias, up_bias,
    shift_mats, spread, crop_rows, inverse,
    box, first, act, grouped, branch, short, y1, pooled, hidden_pre, gating,
    grouped_act, high, low, wide, excited, parts, from_core, from_y, hidden_box,
    send, recv, local,
):
    me = lax.axis_index("chan")
    greet(me)
    link = Link(send, recv)
    copies, beside, passed = [], [], []
    order = (3, 2, 1, 0)
    for p in order:
        mine = pltpu.make_async_copy(own_hbm.at[p], box.at[me, p], local.at[p])
        mine.start()
        theirs = pltpu.make_async_copy(across_hbm.at[p], box.at[me ^ 2, p], local.at[4 + p])
        theirs.start()
        copies.append((mine, theirs))
        beside.append(link.to(own_hbm.at[p], box.at[me, p], me ^ 1))
        passed.append(link.to(across_hbm.at[p], box.at[me ^ 2, p], me ^ 1))
    grouped[...] = jnp.zeros(grouped.shape, F32)
    for at, p in enumerate(order):
        copies[at][0].wait()
        copies[at][1].wait()
        beside[at].wait_recv()
        passed[at].wait_recv()
        total = dot(box[0, p], wa[0])
        for chunk in range(1, NCH):
            total += dot(box[chunk, p], wa[chunk])
        first[p] = total

        def activate(rows, carry):
            act[p, rows] = silu(gains[0:1] * first[p, rows] + moves[0:1]).astype(BF)
            return carry

        by_rows(activate)
        conv_forward(STRIDED_TAPS[p], act, kernel, shift_mats, grouped)
    k = dict(
        gains=gains, moves=moves, grouped=grouped, crop_rows=crop_rows, inverse=inverse,
        pooled=pooled, down=down, up=up, down_bias=down_bias, up_bias=up_bias,
        hidden_pre=hidden_pre, gating=gating, spread=spread, excited=excited,
    )
    s = dict(grouped_act=grouped_act, high=high, low=low, hidden_box=hidden_box, wide=wide)
    steps = excite(link, me, k, s)
    next(steps)
    total = dot(box[0, 0], wp[0])
    for chunk in range(1, NCH):
        total += dot(box[chunk, 0], wp[chunk])
    short[...] = total
    next(steps, None)
    started, passing = scatter_product(link, me, excited, wc, parts, from_core, from_y, wide)
    scatter_end(started, passing)

    def leave(rows, carry):
        total = (
            parts[me, rows].astype(F32) + from_core[1, rows].astype(F32)
        ) + from_y[rows].astype(F32)
        branch[rows] = total
        preact = gains[2:3] * total + moves[2:3] + gains[3:4] * short[rows] + moves[3:4]
        y1[rows] = silu(preact).astype(BF)
        return carry

    by_rows(leave)
    link.finish()


UNIT_TAPS = tuple((tap, 0, tap) for tap in range(9))


def forward_two(
    y1, wa, wc, kernel, down, up, gains, moves, down_bias, up_bias, protos, live, target,
    shift_mats, spread, crop_rows, inverse,
    box, first, act, grouped, branch, pooled, hidden_pre, gating, block_out, loss, dm, dbranch, vector,
    grouped_act, high, low, wide, excited, parts, from_core, from_y, hidden_box,
    score_box, square_box, send, recv,
):
    me = lax.axis_index("chan")
    box[me] = y1[...]
    greet(me)
    link = Link(send, recv)
    gather_chunks(link, me, box)
    total = dot(box[0], wa[0])
    for chunk in range(1, NCH):
        total += dot(box[chunk], wa[chunk])
    first[...] = total
    grouped[...] = jnp.zeros(grouped.shape, F32)

    def activate(rows, carry):
        act[0, rows] = silu(gains[0:1] * first[rows] + moves[0:1]).astype(BF)
        return carry

    by_rows(activate)

    def one_tap(tap, carry):
        moved = dot(shift_mats[tap], act[0]).astype(BF)
        grouped[...] += dot(moved, kernel[tap])
        return carry

    lax.fori_loop(0, 9, one_tap, 0)
    k = dict(
        gains=gains, moves=moves, grouped=grouped, crop_rows=crop_rows, inverse=inverse,
        pooled=pooled, down=down, up=up, down_bias=down_bias, up_bias=up_bias,
        hidden_pre=hidden_pre, gating=gating, spread=spread, excited=excited,
    )
    s = dict(grouped_act=grouped_act, high=high, low=low, hidden_box=hidden_box, wide=wide)
    steps = excite(link, me, k, s)
    next(steps)
    next(steps, None)
    started, passing = scatter_product(link, me, excited, wc, parts, from_core, from_y, wide)
    scatter_end(started, passing)

    def leave(rows, carry):
        total = (
            parts[me, rows].astype(F32) + from_core[1, rows].astype(F32)
        ) + from_y[rows].astype(F32)
        branch[rows] = total
        preact = gains[2:3] * total + moves[2:3] + y1[rows].astype(F32)
        wide[rows] = preact
        y2 = silu(preact)
        grouped_act[rows] = y2
        block_out[rows] = y2.astype(BF)
        return carry

    by_rows(leave)
    emb = pool(crop_rows, inverse, grouped_act, high, low)
    score_box[me] = dot2(emb, protos[...]).astype(BF)
    square_box[me] = jnp.broadcast_to(
        jnp.sum(emb * emb, axis=1, keepdims=True), square_box.shape[1:]
    )
    terms = sum_small(link, me, score_box) + sum_small(link, me, square_box)
    for term in terms:
        term.wait_recv()
    raw = (score_box[0].astype(F32) + score_box[1].astype(F32)) + (
        score_box[2].astype(F32) + score_box[3].astype(F32)
    )
    squares = (square_box[0] + square_box[1] + square_box[2] + square_box[3])[:, :1]
    inv_norm = lax.rsqrt(squares + 1e-6)
    inv_scale = inv_norm * (1.0 / SHARPNESS)
    scores = raw * inv_scale
    onehot = (
        lax.broadcasted_iota(jnp.int32, scores.shape, 1) == target[:, :1]
    ).astype(F32)
    top = jnp.max(scores, axis=1, keepdims=True)
    powers = jnp.exp(scores - top)
    mass = jnp.sum(powers, axis=1, keepdims=True)
    entropy = top + jnp.log(mass) - jnp.sum(onehot * scores, axis=1, keepdims=True)
    alive = live[:, :1]
    loss[...] = jnp.broadcast_to(alive * entropy, loss.shape)
    dscores = LOSS_SCALE * alive * (powers / mass - onehot)
    along = jnp.sum(dscores * scores, axis=1, keepdims=True)
    demb = dot2_nt(dscores, protos[...]) * inv_scale - along * inv_norm * inv_norm * emb
    high[...] = dot2_rows(spread, demb * inverse[:, :1], dm)

    def back(rows, carry):
        masked = dm[rows] * silu_slope(wide[rows])
        dm[rows] = masked
        dbranch[rows] = (gains[2:3] * masked).astype(BF)
        return carry[0] + colsum(masked * branch[rows]), carry[1] + colsum(masked)

    zero = jnp.zeros((1, dm.shape[1]), F32)
    gain_grad, shift_grad = by_rows(back, (zero, zero))
    vector[0:1] = gain_grad
    vector[1:2] = shift_grad
    link.finish()


def dot2_rows(spread, v, out):
    out[...] = spread_rows(spread[...], v)
    return jnp.zeros(out.shape, BF)


PAD = 512


def fold_groups(full, columns_group):
    total = jnp.zeros((GW, full.shape[1]), F32)
    for group in range(full.shape[0] // GW):
        total = total + jnp.where(
            columns_group == group, full[group * GW : (group + 1) * GW], 0.0
        )
    return total


def backward(
    strided,
    box_in, dy, branch, short, vector_in, wa, wp, wc, kernel, down, up, gains, moves, first, act, grouped,
    pooled, hidden_pre, gating, shift_mats, spread, crop_rows, inverse,
    flat, dx,
    dbox, dshort, dexcited, grouped_act, wide, excited, dgrouped, dact, dfirst, hidden_box,
    parts, from_core, from_y, chunks, grad_kernel, local, send, recv,
):
    phases = 4 if strided else 1
    C = wide.shape[1]
    me = lax.axis_index("chan")
    loads = [
        pltpu.make_async_copy(box_in.at[chunk], chunks.at[chunk % 2], local.at[chunk])
        for chunk in range(NCH)
    ]
    loads[0].start()
    loads[1].start()
    zero = jnp.zeros((1, C), F32)
    if strided:

        def head(rows, carry):
            preact = (
                gains[2:3] * branch[rows] + moves[2:3] + gains[3:4] * short[rows] + moves[3:4]
            )
            masked = dy[rows] * silu_slope(preact)
            dbox[me, rows] = (gains[2:3] * masked).astype(BF)
            dshort[rows] = (gains[3:4] * masked).astype(BF)
            return (
                carry[0] + colsum(masked * branch[rows]),
                carry[1] + colsum(masked * short[rows]),
                carry[2] + colsum(masked),
            )

        gain_last, gain_short, shift_last = by_rows(head, (zero, zero, zero))
        shift_short = shift_last
    else:
        dbox[me] = branch[...]
        gain_last, shift_last = vector_in[0:1], vector_in[1:2]
        gain_short, shift_short = zero, zero
    greet(me)
    link = Link(send, recv)
    gather_chunks(link, me, dbox)
    total = dot_nt(dbox[0], wc[0])
    for chunk in range(1, NCH):
        total += dot_nt(dbox[chunk], wc[chunk])
    dexcited[...] = total
    wide[...] = spread_rows(spread[...], gating[...])

    def gate(rows, carry):
        value = silu(gains[1:2] * grouped[rows] + moves[1:2])
        excited[rows] = (value * wide[rows]).astype(BF)
        grouped_act[rows] = dexcited[rows] * value
        return carry

    by_rows(gate)
    ones = jnp.ones((SLOTS, 128), F32)
    dgating = pool(crop_rows, ones, grouped_act, dgrouped, dfirst.at[0])
    gates = gating[...]
    gate_pre = dgating * gates * (1.0 - gates)
    hidden_box[me] = dot2_nt(gate_pre, up[...])
    terms = sum_small(link, me, hidden_box)
    tail = jnp.zeros((PAD - C, C), F32)

    def put(chunk, value, last=tail):
        flat[chunk * PAD : (chunk + 1) * PAD] = jnp.concatenate([value, last]).astype(BF)

    for chunk in range(NCH):
        put(4 + chunk, dot_tn(excited[...], dbox[chunk]))
    for term in terms:
        term.wait_recv()
    hidden_grad = (hidden_box[0] + hidden_box[1] + hidden_box[2] + hidden_box[3]) * silu_slope(
        hidden_pre[...]
    )
    dpooled = dot2_nt(hidden_grad, down[...]) * inverse[:, :1]
    grouped_act[...] = spread_rows(spread[...], dpooled)

    def outer(a, b):
        a_high, a_low = halves(a)
        b_high, b_low = halves(b)
        return dot_tn(a_high, b_high) + dot_tn(a_low, b_high) + dot_tn(a_high, b_low)

    put(9, outer(pooled[...], hidden_grad))
    put(10, outer(silu(hidden_pre[...]), gate_pre))

    def through(rows, carry):
        value = grouped[rows]
        grad = (dexcited[rows] * wide[rows] + grouped_act[rows]) * silu_slope(
            gains[1:2] * value + moves[1:2]
        )
        dgrouped[rows] = (gains[1:2] * grad).astype(BF)
        return carry[0] + colsum(grad * value), carry[1] + colsum(grad)

    gain_mid, shift_mid = by_rows(through, (zero, zero))
    bias_up = colsum(gate_pre)
    bias_down = colsum(hidden_grad)
    columns_group = lax.broadcasted_iota(jnp.int32, (GW, C), 1) // GW
    for p in range(phases):
        dact[p] = jnp.zeros(dact.shape[1:], F32)
    if strided:
        for p in range(phases):
            for tap, phase, move in STRIDED_TAPS[p]:
                if move is None:
                    back = dgrouped[...]
                else:
                    back = dot(shift_mats[move], dgrouped[...]).astype(BF)
                dact[phase] += dot_nt(back, kernel[tap])
                grad_kernel[tap] = fold_groups(dot_tn(act[phase], back), columns_group)
    else:

        def one_tap(tap, carry):
            back = dot(shift_mats[8 - tap], dgrouped[...]).astype(BF)
            dact[0] += dot_nt(back, kernel[tap])
            grad_kernel[tap] = fold_groups(dot_tn(act[0], back), columns_group)
            return carry

        lax.fori_loop(0, 9, one_tap, 0)
    put(8, jnp.concatenate([grad_kernel[tap] for tap in range(9)]))
    sums = (zero, zero)
    for p in range(phases):

        def enter(rows, carry):
            value = first[p, rows]
            grad = dact[p, rows] * silu_slope(gains[0:1] * value + moves[0:1])
            dfirst[p, rows] = (gains[0:1] * grad).astype(BF)
            return carry[0] + colsum(grad * value), carry[1] + colsum(grad)

        sums = by_rows(enter, sums)
    waits = []
    for p in range(phases):
        started, passing = [], []
        mine, core, far = parts.at[p], from_core.at[p], from_y.at[p]
        for h in range(PIECES):
            for chunk in range(NCH):
                total = dot_nt(dfirst[p, piece(h)], wa[chunk])
                if strided and p == 0:
                    total += dot_nt(dshort[piece(h)], wp[chunk])
                mine[chunk, piece(h)] = total.astype(BF)
            started.append(scatter_start(link, me, mine, core, h))
        for h in range(PIECES):
            passing.append(scatter_pass(link, me, mine, core, far, h, started[h]))
        waits.append((started, passing))
    lasts = [
        jnp.concatenate(
            [sums[0], gain_mid, gain_last, gain_short, sums[1], shift_mid, shift_last, shift_short]
        ),
        jnp.concatenate([bias_down, bias_up] + [zero] * 6),
        tail,
        tail,
    ]
    for chunk in range(NCH):
        loads[chunk].wait()
        held = chunks.at[chunk % 2]
        total = dot_tn(held[0], dfirst[0])
        for p in range(1, phases):
            total += dot_tn(held[p], dfirst[p])
        put(chunk, total, lasts[chunk])
        if strided:
            put(11 + chunk, dot_tn(held[0], dshort[...]))
        if chunk + 2 < NCH:
            loads[chunk + 2].start()
    for started, passing in waits:
        scatter_end(started, passing)
    for p in range(phases):

        def leave(rows, carry):
            total = (
                parts[p, me, rows].astype(F32) + from_core[p, 1, rows].astype(F32)
            ) + from_y[p, rows].astype(F32)
            if not strided:
                total = total + dy[rows]
            dx[p, rows] = total.astype(dx.dtype)
            return carry

        by_rows(leave)
    link.finish()


RING = 8


def ring_sum(flat_a, flat_b, out_a, out_b, slots_a, slots_b, send, recv):
    me = lax.axis_index("dp")
    x, z = me % 2, me // 2
    pos = (1 - x) * z + x * (7 - z)

    def device(at):
        at = at % RING
        side = at // 4
        return ((1 - side) * at + side * (7 - at)) * 2 + side

    ahead, behind = device(pos + 1), device(pos + 7)
    barrier = pltpu.get_barrier_semaphore()
    for other in (ahead, behind):
        pl.semaphore_signal(barrier, inc=1, device_id={"dp": other}, device_id_type=MESH)
    pl.semaphore_wait(barrier, 2)
    used = 0
    flying = []

    def put(src, dst, peer):
        nonlocal used
        copy = pltpu.make_async_remote_copy(
            src_ref=src, dst_ref=dst, send_sem=send.at[used], recv_sem=recv.at[used],
            device_id={"dp": peer}, device_id_type=MESH,
        )
        used += 1
        copy.start()
        flying.append(copy)
        return copy

    streams = []
    for flat, out, slots in ((flat_a, out_a, slots_a), (flat_b, out_b, slots_b)):
        size = flat.shape[0] // (2 * RING)
        for way, peer in ((1, ahead), (-1, behind)):
            first = 0 if way == 1 else RING
            box = slots.at[first // RING]

            def rows(block, size=size, first=first):
                return pl.ds(pl.multiple_of((first + (block + 2 * RING) % RING) * size, 16), size)

            streams.append((flat, out, box, size, rows, way, peer))
    last = []
    for flat, out, box, size, rows, way, peer in streams:
        last.append(put(flat.at[rows(pos)], box.at[0], peer))
    for step in range(1, RING):
        for at, (flat, out, box, size, rows, way, peer) in enumerate(streams):
            last[at].wait_recv()
            block = pos - way * step
            base = rows(block).start
            final = step == RING - 1

            def add(i, carry):
                near = pl.ds(pl.multiple_of(base + i * 32, 16), 32)
                here = pl.ds(pl.multiple_of(i * 32, 32), 32)
                total = (box[step - 1, here].astype(F32) + flat[near].astype(F32)).astype(BF)
                if final:
                    out[near] = total
                else:
                    box[step - 1, here] = total
                return carry

            lax.fori_loop(0, size // 32, add, 0)
            if final:
                last[at] = put(out.at[rows(block)], out.at[rows(block)], peer)
            else:
                last[at] = put(box.at[step - 1], box.at[step], peer)
    for step in range(1, RING):
        for at, (flat, out, box, size, rows, way, peer) in enumerate(streams):
            last[at].wait_recv()
            if step < RING - 1:
                block = pos + way - way * step
                last[at] = put(out.at[rows(block)], out.at[rows(block)], peer)
    for copy in flying:
        copy.wait_send()


def vm():
    return pl.BlockSpec(memory_space=pltpu.VMEM)


def shape(dims, dtype=F32):
    return jax.ShapeDtypeStruct(dims, dtype)


def params(number):
    if number is None:
        return pltpu.CompilerParams(vmem_limit_bytes=VMEM_LIMIT)
    return pltpu.CompilerParams(
        vmem_limit_bytes=VMEM_LIMIT, collective_id=number, has_side_effects=True
    )


def call(kernel, number, ins, specs, outs, scratch):
    return pl.pallas_call(
        kernel,
        out_shape=outs,
        in_specs=specs,
        out_specs=[vm()] * len(outs),
        scratch_shapes=scratch,
        compiler_params=params(number),
    )(*ins)


def sems(n):
    return pltpu.SemaphoreType.DMA((n,))


def small(rows, width, dtype):
    return pltpu.VMEM((rows, width), dtype)


def dense_kernel(kernel):
    width = kernel.shape[-1]
    groups = width // GW
    tiled = jnp.tile(kernel, (1, groups, 1))
    row = lax.broadcasted_iota(jnp.int32, (width, width), 0) // GW
    col = lax.broadcasted_iota(jnp.int32, (width, width), 1) // GW
    return jnp.where((row == col)[None], tiled, jnp.zeros((), kernel.dtype))


def per_device(
    pixels, wa1, wb1, se_down1, se_bias1, se_up1, se_gate_bias1, wc1, wp1, scales1, shifts1,
    wa2, wb2, se_down2, se_bias2, se_up2, se_gate_bias2, wc2, scales2, shifts2,
    prototypes, live_counts, crop_image, codes,
):
    C = pixels.shape[1]
    D = wa1.shape[0]
    order = pixel_order()
    spread_np, inverse_np = crop_tables()
    tables_np = shift_tables()
    shift_mats = jnp.asarray(tables_np, BF)
    ahead = jnp.asarray(tables_np[[m for m in STRIDED_MOVES]], BF)
    behind = jnp.asarray(tables_np[[8 - m for m in STRIDED_MOVES]], BF)
    spread = jnp.asarray(spread_np, BF)
    crop_rows = jnp.asarray(spread_np.T.copy(), BF)
    inverse = jnp.asarray(inverse_np, F32)
    place = jnp.asarray(order)[:, None] == jnp.arange(ROWS_IN, dtype=jnp.int32)[None, :]
    place = place.astype(BF)
    own = jnp.dot(place, pixels, preferred_element_type=F32).astype(BF).reshape(4, R, C)
    across = lax.ppermute(own, "chan", [(c, c ^ 2) for c in range(NCH)])
    rows4 = lambda w: w.reshape(NCH, C, C)
    cols4 = lambda w: w.reshape(C, NCH, C).transpose(1, 0, 2)
    line = lambda v: v.reshape(1, -1)
    wa1r, wp1r, wa2r = rows4(wa1), rows4(wp1), rows4(wa2)
    wc1r, wc2r = cols4(wc1), cols4(wc2)
    kernel1, kernel2 = dense_kernel(wb1), dense_kernel(wb2)
    bias = [line(v) for v in (se_bias1, se_gate_bias1, se_bias2, se_gate_bias2)]
    field = small(R, C, F32)
    low = small(R, C, BF)
    comm = [
        pltpu.VMEM((NCH, R, C), BF),
        pltpu.VMEM((2, R, C), BF),
        low,
        pltpu.VMEM((NCH, SLOTS, C), F32),
    ]
    any_ = pl.BlockSpec(memory_space=pl.ANY)
    ins = (
        own, across, wa1r, wp1r, wc1r, kernel1, se_down1, se_up1, scales1, shifts1, bias[0], bias[1],
        ahead, spread, crop_rows, inverse,
    )
    box1, first1, act1, grouped1, branch1, short1, y1, pooled1, hidden_pre1, gating1 = call(
        forward_one, 0, ins, [any_] * 2 + [vm()] * 14,
        [
            shape((NCH, 4, R, C), BF), shape((4, R, C)), shape((4, R, C), BF), shape((R, C)),
            shape((R, C)), shape((R, C)), shape((R, C), BF), shape((SLOTS, C)), shape((SLOTS, C)),
            shape((SLOTS, C)),
        ],
        [field, low, low, field, low] + comm + [sems(24), sems(24), sems(8)],
    )
    lives = jnp.concatenate(
        [
            (jnp.arange(count, dtype=jnp.int32) < live_counts[bucket]).astype(F32)
            for bucket, count in enumerate(COUNTS)
        ]
        + [jnp.zeros((SLOTS - CROPS,), F32)]
    )
    match = crop_image[:, None] == jnp.arange(codes.shape[0], dtype=jnp.int32)[None, :]
    target = jnp.pad(jnp.sum(jnp.where(match, codes[None, :], 0), axis=1), (0, SLOTS - CROPS))
    lives = jnp.broadcast_to(lives[:, None], (SLOTS, 128))
    target = jnp.broadcast_to(target[:, None], (SLOTS, 128)).astype(jnp.int32)
    protos = prototypes.shape[1]
    ins = (
        y1, wa2r, wc2r, kernel2, se_down2, se_up2, scales2, shifts2, bias[2], bias[3], prototypes,
        lives, target, shift_mats, spread, crop_rows, inverse,
    )
    (
        box2, first2, act2, grouped2, branch2, pooled2, hidden_pre2, gating2, block_out, loss, dm2, dbranch2,
        vector2,
    ) = call(
        forward_two, 1, ins, [vm()] * 17,
        [
            shape((NCH, R, C), BF), shape((R, C)), shape((1, R, C), BF), shape((R, C)), shape((R, C)),
            shape((SLOTS, C)), shape((SLOTS, C)), shape((SLOTS, C)), shape((R, C), BF),
            shape((SLOTS, 128)), shape((R, C)), shape((R, C), BF), shape((8, C)),
        ],
        [field, low, low, field, low] + comm
        + [
            pltpu.VMEM((NCH, SLOTS, protos), BF), pltpu.VMEM((NCH, SLOTS, 128), F32),
            sems(32), sems(32),
        ],
    )
    hidden_box = pltpu.VMEM((NCH, SLOTS, C), F32)

    def back(number, strided, ins):
        n = 4 if strided else 1
        total = 15 if strided else 11
        outs = [shape((total * PAD, C), BF), shape((n, R, C), BF if strided else F32)]
        scratch = [
            pltpu.VMEM((NCH, R, C), BF), low if strided else small(16, 128, BF), field, field,
            field, low, low, pltpu.VMEM((n, R, C), F32), pltpu.VMEM((n, R, C), BF), hidden_box,
            pltpu.VMEM((n, NCH, R, C), BF), pltpu.VMEM((n, 2, R, C), BF), pltpu.VMEM((n, R, C), BF),
            pltpu.VMEM((2, n, R, C), BF), pltpu.VMEM((9, GW, C), F32), sems(NCH), sems(40), sems(40),
        ]
        return call(
            functools.partial(backward, strided), number, ins, [any_] + [vm()] * (len(ins) - 1), outs, scratch
        )

    tables = (spread, crop_rows, inverse)
    flat2, dy1 = back(
        2, False,
        (
            box2[:, None], dm2, dbranch2, vector2, vector2, wa2r, vector2, wc2r, kernel2, se_down2, se_up2,
            scales2, shifts2, first2[None], act2, grouped2, pooled2, hidden_pre2, gating2, shift_mats,
        )
        + tables,
    )
    flat1, dx = back(
        3, True,
        (
            box1, dy1[0], branch1, short1, vector2, wa1r, wp1r, wc1r, kernel1, se_down1, se_up1, scales1,
            shifts1, first1, act1, grouped1, pooled1, hidden_pre1, gating1, behind,
        )
        + tables,
    )
    flat_dx = dx.reshape(4 * R, C)
    pixels_grad = lax.dot_general(
        place, flat_dx, (((0,), (0,)), ((), ())), preferred_element_type=F32
    ).astype(BF)
    if lax.axis_size("dp") == RING:
        blocks = [f.shape[0] // (2 * RING) for f in (flat1, flat2)]
        sum1, sum2 = call(
            ring_sum, 4, (flat1, flat2), [vm()] * 2, [shape(flat1.shape, BF), shape(flat2.shape, BF)],
            [pltpu.VMEM((2, RING - 1, n, C), BF) for n in blocks] + [sems(56), sems(56)],
        )
    else:
        sum1, sum2 = lax.psum((flat1, flat2), "dp")

    def unpack(total):
        piece = lambda at: total[at * PAD : at * PAD + C].astype(F32)
        rows = lambda at: jnp.concatenate([piece(at + i) for i in range(NCH)])
        cols = lambda at: jnp.concatenate([piece(at + i) for i in range(NCH)], axis=1)
        first = total[C:PAD].astype(F32)
        second = total[PAD + C : 2 * PAD].astype(F32)
        return rows, cols, piece, first, second

    rows_1, cols_1, piece_1, first_v1, second_v1 = unpack(sum1)
    rows_2, cols_2, piece_2, first_v2, second_v2 = unpack(sum2)
    return (
        block_out[:ROWS],
        loss[:CROPS, 0],
        pixels_grad,
        rows_1(0),
        piece_1(8).reshape(9, GW, C),
        piece_1(9),
        second_v1[0],
        piece_1(10),
        second_v1[1],
        cols_1(4),
        rows_1(11),
        first_v1[:4],
        first_v1[4:],
        rows_2(0),
        piece_2(8).reshape(9, GW, C),
        piece_2(9),
        second_v2[0],
        piece_2(10),
        second_v2[1],
        cols_2(4),
        first_v2[:3],
        first_v2[4:7],
    )


def solution(mesh):
    col, row, deep, whole = P(None, "chan"), P("chan", None), P(None, None, "chan"), P()
    one = (col, deep, row, whole, col, P("chan"), row, col, col, col)
    two = (col, deep, row, whole, col, P("chan"), row, col, col)
    return jax.shard_map(
        per_device,
        mesh=mesh,
        in_specs=(P("dp", "chan"), *one, *two, row, P("dp"), P("dp"), P("dp")),
        out_specs=(P("dp", "chan"), P("dp"), P("dp", "chan"), *one, *two),
        check_vma=False,
    )
```
